32 devices in a mesh: ens: 2 (over x), lon: 4 (over y, core), lat: 4 (over z).
Axes of the slice: x: 2, y: 2, z: 4, core: 2. Of those that a mesh axis runs over, the one named last changes fastest.
Arguments:
- fields: bfloat16 [8, 768, 1024], P(('ens', 'lat'), 'lon'), parts along dimension 0, may hold values from -6 to 6
- conv_weight: bfloat16 [9216, 1024], P(None, 'lon'), may hold values from -0.0625 to 0.0625
- norm_gain: float32 [1024], replicated, may hold values from 0.1 to 1.9
- qkv_weight: bfloat16 [1024, 3072], replicated, may hold values from -0.1875 to 0.1875
- out_weight: bfloat16 [1024, 1024], replicated, may hold values from -0.1875 to 0.1875
- key_bias: bfloat16 [4, 768, 16], P('lat', 'lon'), may hold values from -8 to 250
Outputs:
- mixed: bfloat16 [8, 768, 1024], P(('ens', 'lat'), 'lon'), parts along dimension 0
The draws below stay inside these ranges and needn't reach their ends.
There are 2 independent parts, one for each index of `ens`. The reference program is written for one: setup_inputs(seed, part) draws one part's arguments, and reference() takes and returns one part's arrays. A program takes and returns all parts, laid end to end along the dimension named above; an argument that names none is the same for every part. Nothing has to cross between parts.
All inputs are finite; a program needn't handle non-finite values.
Results may differ from the reference program's by a relative error of at most 0.012.
Values may be sent and summed in bfloat16 or wider, within the bound.
A program may use at most 128 MiB of HBM per device.

```python
import jax
import jax.numpy as jnp
from jax import lax

D = 1024
H = 16
NLAT = 4
NLON = 768


def draw_key_bias(key, part):
    first = jax.random.fold_in(key, 0)
    values = jnp.clip(2.0 * jax.random.normal(first, (NLAT, NLON, H), jnp.float32), -8.0, 8.0)
    return values.astype(jnp.bfloat16)


def shard_levels(own_key, shape, pieces, smallest, largest):
    factor_of = 1.0
    for position, parts in pieces:
        steps = jax.random.uniform(jax.random.fold_in(jax.random.fold_in(own_key, 6), position), (parts,), jnp.float32, smallest / len(pieces), largest / len(pieces))
        factor_of = factor_of * jnp.repeat(jnp.exp(steps), shape[position] // parts).reshape((-1,) + (1,) * (len(shape) - 1 - position))
    return factor_of


def centred(key, extent, scale, most, shards=(), kind=jnp.bfloat16):
    factor_of = shard_levels(key, extent, shards, -0.22, 0.18) if shards else 1.0
    drawn = jax.random.normal(key, extent, jnp.float32) * scale * factor_of
    return jnp.minimum(jnp.maximum(drawn, -most), most).astype(kind)


def setup_inputs(seed: int = 0, part: int = 0) -> dict:
    key_list = jax.random.split(jax.random.key(seed), 7)
    own_keys = jax.random.split(jax.random.fold_in(key_list[6], part), 7)
    fields = centred(own_keys[0], (NLAT, NLON, D), 1.0, 6.0, ((0, 4), (1, 4)))
    conv_weight = centred(key_list[1], (9 * D, D), (9 * D) ** -0.5, 0.0625, ((1, 4),))
    norm_gain = jnp.clip(1.0 + 0.18 * jax.random.normal(key_list[2], (D,), jnp.float32), 0.1, 1.9)
    qkv_weight = centred(key_list[3], (D, 3 * D), D ** -0.5, 0.1875)
    out_weight = centred(key_list[4], (D, D), D ** -0.5, 0.1875)
    key_bias = draw_key_bias(jax.random.fold_in(key_list[6], 71), part)
    return dict(fields=fields, conv_weight=conv_weight, norm_gain=norm_gain, qkv_weight=qkv_weight, out_weight=out_weight, key_bias=key_bias)


def one_row(row_parts):
    query_row, key_row, value_row, bias_row = row_parts
    head_dim = D // H
    query_heads = query_row.reshape(NLON, H, head_dim).astype(jnp.float32)
    key_heads = key_row.reshape(NLON, H, head_dim).astype(jnp.float32)
    value_heads = value_row.reshape(NLON, H, head_dim).astype(jnp.float32)
    scores = jnp.einsum('qhd,khd->hqk', query_heads, key_heads) / jnp.sqrt(jnp.float32(head_dim))
    scores = scores + jnp.transpose(bias_row.astype(jnp.float32))[:, None, :]
    best = lax.optimization_barrier(jnp.max(scores, axis=-1, keepdims=True))
    weights = jnp.exp(scores - best)
    totals = lax.optimization_barrier(jnp.sum(weights, axis=-1))
    rounded = weights.astype(jnp.bfloat16).astype(jnp.float32)
    summed = jnp.einsum('hqk,khd->qhd', rounded, value_heads)
    result = summed / jnp.transpose(totals)[:, :, None]
    return result.reshape(NLON, D).astype(jnp.bfloat16)

def reference(fields, conv_weight, norm_gain, qkv_weight, out_weight, key_bias):
    banded = jnp.pad(fields, ((1, 1), (0, 0), (0, 0)))
    wrapped = jnp.concatenate([banded[:, -1:], banded, banded[:, :1]], axis=1)
    accum = jnp.zeros((NLAT * NLON, D), jnp.float32)
    tap_idx = 0
    for step_lat in (-1, 0, 1):
        for step_lon in (-1, 0, 1):
            shifted = wrapped[1 + step_lat:1 + step_lat + NLAT, 1 + step_lon:1 + step_lon + NLON].reshape(NLAT * NLON, D)
            accum = accum + jnp.dot(shifted, conv_weight[tap_idx * D:(tap_idx + 1) * D], preferred_element_type=jnp.float32)
            tap_idx += 1
    conv_out = accum.astype(jnp.bfloat16)
    residual = (fields.reshape(NLAT * NLON, D).astype(jnp.float32) + conv_out.astype(jnp.float32)).astype(jnp.bfloat16)
    stream = residual.astype(jnp.float32)
    normed = (stream * lax.rsqrt(lax.optimization_barrier(jnp.mean(stream * stream, axis=-1, keepdims=True)) + 1e-06) * norm_gain).astype(jnp.bfloat16)
    projected = jnp.dot(normed, qkv_weight, preferred_element_type=jnp.float32).astype(jnp.bfloat16)
    queries = projected[:, :D].reshape(NLAT, NLON, D)
    key_rows = projected[:, D:2 * D].reshape(NLAT, NLON, D)
    value_rows = projected[:, 2 * D:].reshape(NLAT, NLON, D)
    attended = lax.map(one_row, (queries, key_rows, value_rows, key_bias))
    mixed = residual.astype(jnp.float32) + jnp.dot(attended.reshape(NLAT * NLON, D), out_weight, preferred_element_type=jnp.float32)
    return mixed.astype(jnp.bfloat16).reshape(NLAT, NLON, D)
```

```python
import functools
import math

import jax
import jax.numpy as jnp
from jax import lax
from jax.experimental import pallas as pl
from jax.experimental.pallas import tpu as pltpu
from jax.sharding import PartitionSpec as P

H = 16


def extended(block, sides, width):
    for axis, dim in sides:
        count = lax.axis_size(axis)
        forward = [(i, i + 1) for i in range(count - 1)]
        backward = [(target, source) for source, target in forward]
        low = lax.ppermute(
            lax.slice_in_dim(block, block.shape[dim] - width, None, axis=dim), axis, forward
        )
        high = lax.ppermute(lax.slice_in_dim(block, 0, width, axis=dim), axis, backward)
        block = jnp.concatenate([low, block, high], axis=dim)
    return block


def tap_sum(wrapped, conv_weight, out_rows, lon_total, channels):
    out_width = conv_weight.shape[1]
    accum_cols = jnp.zeros((out_rows * lon_total, out_width), jnp.float32)
    tap_idx = 0
    for step_lat in (-1, 0, 1):
        for step_lon in (-1, 0, 1):
            shifted = wrapped[
                1 + step_lat : 1 + step_lat + out_rows, 1 + step_lon : 1 + step_lon + lon_total
            ].reshape(out_rows * lon_total, channels)
            accum_cols = accum_cols + jnp.dot(
                shifted,
                conv_weight[tap_idx * channels : (tap_idx + 1) * channels],
                preferred_element_type=jnp.float32,
            )
            tap_idx += 1
    return accum_cols.reshape(out_rows, lon_total, out_width)


def on_device(fields, conv_weight, norm_gain, qkv_weight, out_weight, key_bias):
    lat_n, lon_n, channels = fields.shape
    row_count = lat_n * lon_n
    head_dim = channels // H
    score_scale = 1.0 / math.sqrt(head_dim)
    banded = extended(fields, (("lat", 0),), 1)
    circle = lax.all_gather(banded, "lon", axis=1, tiled=True)
    lon_total = circle.shape[1]
    wrapped = jnp.concatenate([circle[:, -1:], circle, circle[:, :1]], axis=1)
    out_cols = tap_sum(wrapped, conv_weight, lat_n, lon_total, channels).astype(jnp.bfloat16)
    conv_out = lax.all_to_all(out_cols, "lon", split_axis=1, concat_axis=2, tiled=True).reshape(
        row_count, channels
    )
    residual = (
        fields.reshape(row_count, channels).astype(jnp.float32) + conv_out.astype(jnp.float32)
    ).astype(jnp.bfloat16)
    stream = residual.astype(jnp.float32)
    normed = (
        stream * lax.rsqrt(jnp.mean(stream * stream, axis=-1, keepdims=True) + 1e-06) * norm_gain
    ).astype(jnp.bfloat16)
    projected = jnp.dot(normed, qkv_weight, preferred_element_type=jnp.float32).astype(jnp.bfloat16)
    queries = projected[:, :channels].reshape(lat_n, lon_n, channels)
    key_rows = projected[:, channels : 2 * channels].reshape(lat_n, lon_n, channels)
    value_rows = projected[:, 2 * channels :].reshape(lat_n, lon_n, channels)
    query_heads = queries.reshape(lat_n, lon_n, H, head_dim)
    best = jnp.full((lat_n, H, lon_n), -1e30, jnp.float32)
    key_part = lax.all_gather(key_rows, "lon", axis=1, tiled=True)
    value_part = lax.all_gather(value_rows, "lon", axis=1, tiled=True)
    bias_part = lax.all_gather(key_bias, "lon", axis=1, tiled=True)
    span = key_part.shape[1]
    key_heads = key_part.reshape(lat_n, span, H, head_dim)
    value_heads = value_part.reshape(lat_n, span, H, head_dim)
    scores = (
        jnp.einsum("aqhd,akhd->ahqk", query_heads, key_heads, preferred_element_type=jnp.float32)
        * score_scale
    )
    scores = scores + jnp.transpose(bias_part, (0, 2, 1)).astype(jnp.float32)[:, :, None, :]
    new_best = jnp.maximum(best, jnp.max(scores, axis=-1))
    weights = jnp.exp(scores - new_best[..., None])
    denom = jnp.sum(weights, axis=-1)
    accum = jnp.einsum(
        "ahqk,akhd->ahqd",
        weights.astype(jnp.bfloat16),
        value_heads,
        preferred_element_type=jnp.float32,
    )
    best, denom, accum = (new_best, denom, accum)
    attended = (
        jnp.transpose(accum / denom[..., None], (0, 2, 1, 3))
        .reshape(row_count, channels)
        .astype(jnp.bfloat16)
    )
    mixed = residual.astype(jnp.float32) + jnp.dot(
        attended, out_weight, preferred_element_type=jnp.float32
    )
    return mixed.astype(jnp.bfloat16).reshape(lat_n, lon_n, channels)


MESH = pl.DeviceIdType.MESH
EDGE = 16
PIECES = 2
OWN_SIB, EDGE_P, EDGE_Q, BIAS_SIB, BIAS_P, BIAS_Q = 0, 1, 2, 3, 4, 5
CONV_P, CONV_SIB, CONV_FWD = 6, 8, 10
UP, DOWN = 12, 14
ATT_P, ATT_Q, ATT_SIB = 16, 17, 18
PIECE, PIECE_FWD = 19, 19 + PIECES
COPIES = 19 + 2 * PIECES


def block_kernel(
    lat_count,
    fields_ref,
    conv_ref,
    gain_ref,
    qkv_ref,
    outw_ref,
    bias_ref,
    out_ref,
    xbuf,
    conv_w,
    qkv_w,
    out_w,
    bias_own,
    bias_all,
    part_send,
    part_recv,
    centre,
    cols,
    resid,
    normed,
    proj,
    att_send,
    att,
    send_sem,
    recv_sem,
    load_sem,
):
    n, channels = fields_ref.shape[1], fields_ref.shape[2]
    width = conv_ref.shape[1]
    half = 2 * n
    blocks = channels // width
    head_dim = channels // H
    me, row = lax.axis_index("lon"), lax.axis_index("lat")
    y, c = me // 2, me % 2
    sib, p, q = 2 * y + 1 - c, 2 * (1 - y) + c, 2 * (1 - y) + 1 - c
    above, below = row > 0, row < lat_count - 1

    def load(src, dst, idx):
        copy = pltpu.make_async_copy(src, dst, load_sem.at[idx])
        copy.start()
        return copy

    def remote(src, dst, idx, target):
        return pltpu.make_async_remote_copy(
            src_ref=src,
            dst_ref=dst,
            send_sem=send_sem.at[idx],
            recv_sem=recv_sem.at[idx],
            device_id=target,
            device_id_type=MESH,
        )

    def rows_at(offset, count):
        return pl.ds(pl.multiple_of(offset, EDGE), count)

    own = fields_ref.at[0]
    loads = [load(own, xbuf.at[0, rows_at(EDGE + c * n, n)], 0)]
    tap_rows = 3 * channels
    for idx, a in ((1, 2), (2, 0), (3, 1)):
        span = pl.ds(a * tap_rows, tap_rows)
        loads.append(load(conv_ref.at[span], conv_w.at[span], idx))
    for j in range(3):
        lanes = pl.ds(pl.multiple_of(j * channels + me * width, width), width)
        loads.append(load(qkv_ref.at[:, lanes], qkv_w.at[j], 4 + j))
    loads.append(load(outw_ref, out_w, 7))

    barrier = pltpu.get_barrier_semaphore()
    for other in (sib, p, q):
        pl.semaphore_signal(barrier, inc=1, device_id={"lon": other}, device_id_type=MESH)

    @pl.when(above)
    def _():
        pl.semaphore_signal(barrier, inc=1, device_id={"lat": row - 1}, device_id_type=MESH)

    @pl.when(below)
    def _():
        pl.semaphore_signal(barrier, inc=1, device_id={"lat": row + 1}, device_id_type=MESH)

    lane = lax.broadcasted_iota(jnp.int32, (H, 2 * head_dim), 1)
    which = lax.broadcasted_iota(jnp.int32, (H, 2 * head_dim), 0)
    spread = jnp.where((lane == which) | (lane == which + head_dim), 1.0, 0.0).astype(jnp.bfloat16)
    bias_own[...] = jnp.dot(bias_ref[0], spread, preferred_element_type=jnp.float32).astype(
        jnp.bfloat16
    )
    bias_all[rows_at(c * n, n)] = bias_own[...]

    pl.semaphore_wait(barrier, 3 + above.astype(jnp.int32) + below.astype(jnp.int32))

    sends = []

    def begin(copy):
        copy.start()
        sends.append(copy)
        return copy

    edge_src = fields_ref.at[0, rows_at(c * (n - EDGE), EDGE)]
    edge_dst = xbuf.at[0, rows_at((1 - c) * (EDGE + half), EDGE)]
    edges = [
        begin(remote(edge_src, edge_dst, EDGE_P, {"lon": p})),
        begin(remote(edge_src, edge_dst, EDGE_Q, {"lon": q})),
    ]
    to_sib = begin(
        remote(own, xbuf.at[0, rows_at(EDGE + c * n, n)], OWN_SIB, {"lon": sib})
    )
    piece = n // PIECES
    pieces = [
        begin(
            remote(
                fields_ref.at[0, pl.ds(g * piece, piece)],
                xbuf.at[1, rows_at(EDGE + c * n + g * piece, piece)],
                PIECE + g,
                {"lon": p},
            )
        )
        for g in range(PIECES)
    ]
    biases = [
        begin(remote(bias_own, bias_all.at[rows_at(c * n, n)], BIAS_SIB, {"lon": sib})),
        begin(remote(bias_own, bias_all.at[rows_at(half + c * n, n)], BIAS_P, {"lon": p})),
        begin(remote(bias_own, bias_all.at[rows_at(half + c * n, n)], BIAS_Q, {"lon": q})),
    ]

    def taps(k, a):
        full = EDGE + half + EDGE
        total = None
        for b in range(3):
            tap = 3 * a + b
            part = jnp.dot(
                xbuf[k],
                conv_w[tap * channels : (tap + 1) * channels],
                preferred_element_type=jnp.float32,
            )
            if b != 1:
                part = pltpu.roll(part, (1 - b) % full, 0)
            total = part if total is None else total + part
        return total[EDGE : EDGE + half]

    up = [
        remote(part_send.at[k, 0], part_recv.at[k, 0], UP + k, {"lat": row - 1}) for k in range(2)
    ]
    down = [
        remote(part_send.at[k, 1], part_recv.at[k, 1], DOWN + k, {"lat": row + 1})
        for k in range(2)
    ]

    def send_up(k):
        part_send[k, 0] = taps(k, 2).astype(jnp.bfloat16)
        pl.when(above)(up[k].start)

    def send_down(k):
        part_send[k, 1] = taps(k, 0).astype(jnp.bfloat16)
        pl.when(below)(down[k].start)

    conv_p = [
        remote(cols.at[k, me], cols.at[1 - k, me], CONV_P + k, {"lon": p}) for k in range(2)
    ]
    conv_sib = [
        remote(cols.at[k, me], cols.at[k, me], CONV_SIB + k, {"lon": sib}) for k in range(2)
    ]
    conv_fwd = [
        remote(cols.at[1 - k, p], cols.at[1 - k, p], CONV_FWD + k, {"lon": sib})
        for k in range(2)
    ]

    def finish_conv(k):
        @pl.when(below)
        def _():
            up[k].wait_recv()
            centre[k] = centre[k] + part_recv[k, 0].astype(jnp.float32)

        @pl.when(above)
        def _():
            down[k].wait_recv()
            centre[k] = centre[k] + part_recv[k, 1].astype(jnp.float32)

        cols[k, me] = centre[k].astype(jnp.bfloat16)
        begin(conv_p[k])
        begin(conv_sib[k])

    loads[0].wait()
    to_sib.wait_recv()
    for copy in edges:
        copy.wait_recv()
    xbuf[1, 0:EDGE] = xbuf[0, half : half + EDGE]
    xbuf[1, EDGE + half : EDGE + half + EDGE] = xbuf[0, EDGE : EDGE + EDGE]
    loads[1].wait()
    send_up(0)
    loads[2].wait()
    send_down(0)
    loads[3].wait()
    centre[0] = taps(0, 1)

    forwards = []
    for g in range(PIECES):
        pieces[g].wait_recv()
        got = xbuf.at[1, rows_at(EDGE + c * n + g * piece, piece)]
        forwards.append(begin(remote(got, got, PIECE_FWD + g, {"lon": sib})))
    finish_conv(0)
    for copy in forwards:
        copy.wait_recv()
    send_up(1)
    send_down(1)
    centre[1] = taps(1, 1)
    conv_p[0].wait_recv()
    begin(conv_fwd[0])
    finish_conv(1)

    for j in range(3):
        loads[4 + j].wait()

    def project(k):
        squares = jnp.zeros((half, 1), jnp.float32)
        for o in range(blocks):
            lanes = slice(o * width, (o + 1) * width)
            summed = (
                xbuf[k, EDGE : EDGE + half, lanes].astype(jnp.float32)
                + cols[k, o].astype(jnp.float32)
            ).astype(jnp.bfloat16)
            resid[k, :, lanes] = summed
            wide = summed.astype(jnp.float32)
            squares = squares + jnp.sum(wide * wide, axis=-1, keepdims=True)
        scale = lax.rsqrt(squares / channels + 1e-06)
        for o in range(blocks):
            lanes = slice(o * width, (o + 1) * width)
            normed[:, lanes] = (
                resid[k, :, lanes].astype(jnp.float32) * scale * gain_ref[:, lanes]
            ).astype(jnp.bfloat16)
        for j in range(3):
            proj[j, k * half : (k + 1) * half] = jnp.dot(
                normed[...], qkv_w[j], preferred_element_type=jnp.float32
            ).astype(jnp.bfloat16)

    conv_sib[1].wait_recv()
    conv_fwd[0].wait_recv()
    project(1)
    conv_p[1].wait_recv()
    begin(conv_fwd[1])
    conv_sib[0].wait_recv()
    conv_fwd[1].wait_recv()
    project(0)
    for copy in biases:
        copy.wait_recv()

    tile = 2 * head_dim
    score_scale = 1.0 / math.sqrt(head_dim)
    low_q = lax.broadcasted_iota(jnp.int32, (n, tile), 1)
    low_k = lax.broadcasted_iota(jnp.int32, (2 * half, tile), 1)

    def attend(offset, dst):
        for pair in range(width // tile):
            lanes = slice(pair * tile, (pair + 1) * tile)
            queries = proj[0, rows_at(offset, n), lanes].astype(jnp.float32) * score_scale
            keys, values = proj[1, :, lanes], proj[2, :, lanes]
            outs = []
            for odd in range(2):
                head = me * (width // head_dim) + 2 * pair + odd
                mine_q = (low_q >= head_dim) if odd else (low_q < head_dim)
                mine_k = (low_k >= head_dim) if odd else (low_k < head_dim)
                picked = jnp.where(low_q == head + (0 if odd else head_dim), 1.0, 0.0)
                q_ext = jnp.where(mine_q, queries, picked).astype(jnp.bfloat16)
                k_ext = jnp.where(mine_k, keys, bias_all[...])
                scores = lax.dot_general(
                    q_ext, k_ext, (((1,), (1,)), ((), ())), preferred_element_type=jnp.float32
                )
                weights = jnp.exp(scores - jnp.max(scores, axis=-1, keepdims=True))
                total = jnp.sum(weights, axis=-1, keepdims=True)
                summed = jnp.dot(
                    weights.astype(jnp.bfloat16), values, preferred_element_type=jnp.float32
                )
                outs.append(summed / total)
            dst[:, lanes] = jnp.where(low_q < head_dim, outs[0], outs[1]).astype(jnp.bfloat16)

    attend(half + (1 - c) * n, att_send.at[0])
    att_q = begin(remote(att_send.at[0], att.at[me], ATT_Q, {"lon": q}))
    attend(half + c * n, att_send.at[1])
    att_p = begin(remote(att_send.at[1], att.at[me], ATT_P, {"lon": p}))
    attend((1 - c) * n, att_send.at[2])
    att_s = begin(remote(att_send.at[2], att.at[me], ATT_SIB, {"lon": sib}))
    attend(c * n, att.at[me])
    loads[7].wait()
    for copy in (att_s, att_q, att_p):
        copy.wait_recv()

    for j in range(blocks):
        lanes = slice(j * width, (j + 1) * width)
        mixed = resid[0, rows_at(c * n, n), lanes].astype(jnp.float32)
        for o in range(blocks):
            mixed = mixed + jnp.dot(
                att[o], out_w[o * width : (o + 1) * width, lanes], preferred_element_type=jnp.float32
            )
        out_ref[0, :, lanes] = mixed.astype(jnp.bfloat16)

    for copy in sends:
        copy.wait_send()
    for k in range(2):
        pl.when(above)(up[k].wait_send)
        pl.when(below)(down[k].wait_send)


def fused(fields, conv_weight, norm_gain, qkv_weight, out_weight, key_bias):
    _, n, channels = fields.shape
    width = conv_weight.shape[1]
    half = 2 * n
    lat_count = lax.axis_size("lat")
    lon_count = lax.axis_size("lon")
    head_dim = channels // H
    bf16, f32 = jnp.bfloat16, jnp.float32
    any_spec = pl.BlockSpec(memory_space=pl.ANY)
    vmem_spec = pl.BlockSpec(memory_space=pltpu.VMEM)
    return pl.pallas_call(
        functools.partial(block_kernel, lat_count),
        out_shape=jax.ShapeDtypeStruct(fields.shape, bf16),
        in_specs=[any_spec, any_spec, vmem_spec, any_spec, any_spec, vmem_spec],
        out_specs=vmem_spec,
        scratch_shapes=[
            pltpu.VMEM((2, half + 2 * EDGE, channels), bf16),
            pltpu.VMEM(conv_weight.shape, bf16),
            pltpu.VMEM((3, channels, width), bf16),
            pltpu.VMEM(out_weight.shape, bf16),
            pltpu.VMEM((n, 2 * head_dim), bf16),
            pltpu.VMEM((2 * half, 2 * head_dim), bf16),
            pltpu.VMEM((2, 2, half, width), bf16),
            pltpu.VMEM((2, 2, half, width), bf16),
            pltpu.VMEM((2, half, width), f32),
            pltpu.VMEM((2, lon_count, half, width), bf16),
            pltpu.VMEM((2, half, channels), bf16),
            pltpu.VMEM((half, channels), bf16),
            pltpu.VMEM((3, 2 * half, width), bf16),
            pltpu.VMEM((3, n, width), bf16),
            pltpu.VMEM((lon_count, n, width), bf16),
            pltpu.SemaphoreType.DMA((COPIES,)),
            pltpu.SemaphoreType.DMA((COPIES,)),
            pltpu.SemaphoreType.DMA((8,)),
        ],
        compiler_params=pltpu.CompilerParams(
            collective_id=0, has_side_effects=True, vmem_limit_bytes=44 * 1024 * 1024
        ),
    )(fields, conv_weight, norm_gain.reshape(1, channels), qkv_weight, out_weight, key_bias)


def suits_kernel(fields, conv_weight):
    lat_n, n, channels = fields.shape
    width = conv_weight.shape[1]
    head_dim = channels // H
    return (
        lat_n == 1
        and lax.axis_size("lon") == 4
        and n % (EDGE * PIECES) == 0
        and width % 128 == 0
        and 2 * head_dim == 128
        and H <= head_dim
        and n * channels <= 2**18
    )


def per_device(fields, conv_weight, *others):
    if suits_kernel(fields, conv_weight):
        return fused(fields, conv_weight, *others)
    return on_device(fields, conv_weight, *others)


def solution(mesh):
    return jax.shard_map(
        per_device,
        mesh=mesh,
        in_specs=(
            P(("ens", "lat"), "lon", None),
            P(None, "lon"),
            P(),
            P(),
            P(),
            P("lat", "lon", None),
        ),
        out_specs=P(("ens", "lat"), "lon", None),
        check_vma=False,
    )
```

```python
import functools
import math

import jax
import jax.numpy as jnp
from jax import lax
from jax.experimental import pallas as pl
from jax.experimental.pallas import tpu as pltpu
from jax.sharding import PartitionSpec as P

H = 16


def extended(block, sides, width):
    for axis, dim in sides:
        count = lax.axis_size(axis)
        forward = [(i, i + 1) for i in range(count - 1)]
        backward = [(target, source) for source, target in forward]
        low = lax.ppermute(
            lax.slice_in_dim(block, block.shape[dim] - width, None, axis=dim), axis, forward
        )
        high = lax.ppermute(lax.slice_in_dim(block, 0, width, axis=dim), axis, backward)
        block = jnp.concatenate([low, block, high], axis=dim)
    return block


def tap_sum(wrapped, conv_weight, out_rows, lon_total, channels):
    out_width = conv_weight.shape[1]
    accum_cols = jnp.zeros((out_rows * lon_total, out_width), jnp.float32)
    tap_idx = 0
    for step_lat in (-1, 0, 1):
        for step_lon in (-1, 0, 1):
            shifted = wrapped[
                1 + step_lat : 1 + step_lat + out_rows, 1 + step_lon : 1 + step_lon + lon_total
            ].reshape(out_rows * lon_total, channels)
            accum_cols = accum_cols + jnp.dot(
                shifted,
                conv_weight[tap_idx * channels : (tap_idx + 1) * channels],
                preferred_element_type=jnp.float32,
            )
            tap_idx += 1
    return accum_cols.reshape(out_rows, lon_total, out_width)


def on_device(fields, conv_weight, norm_gain, qkv_weight, out_weight, key_bias):
    lat_n, lon_n, channels = fields.shape
    row_count = lat_n * lon_n
    head_dim = channels // H
    score_scale = 1.0 / math.sqrt(head_dim)
    banded = extended(fields, (("lat", 0),), 1)
    circle = lax.all_gather(banded, "lon", axis=1, tiled=True)
    lon_total = circle.shape[1]
    wrapped = jnp.concatenate([circle[:, -1:], circle, circle[:, :1]], axis=1)
    out_cols = tap_sum(wrapped, conv_weight, lat_n, lon_total, channels).astype(jnp.bfloat16)
    conv_out = lax.all_to_all(out_cols, "lon", split_axis=1, concat_axis=2, tiled=True).reshape(
        row_count, channels
    )
    residual = (
        fields.reshape(row_count, channels).astype(jnp.float32) + conv_out.astype(jnp.float32)
    ).astype(jnp.bfloat16)
    stream = residual.astype(jnp.float32)
    normed = (
        stream * lax.rsqrt(jnp.mean(stream * stream, axis=-1, keepdims=True) + 1e-06) * norm_gain
    ).astype(jnp.bfloat16)
    projected = jnp.dot(normed, qkv_weight, preferred_element_type=jnp.float32).astype(jnp.bfloat16)
    queries = projected[:, :channels].reshape(lat_n, lon_n, channels)
    key_rows = projected[:, channels : 2 * channels].reshape(lat_n, lon_n, channels)
    value_rows = projected[:, 2 * channels :].reshape(lat_n, lon_n, channels)
    query_heads = queries.reshape(lat_n, lon_n, H, head_dim)
    best = jnp.full((lat_n, H, lon_n), -1e30, jnp.float32)
    key_part = lax.all_gather(key_rows, "lon", axis=1, tiled=True)
    value_part = lax.all_gather(value_rows, "lon", axis=1, tiled=True)
    bias_part = lax.all_gather(key_bias, "lon", axis=1, tiled=True)
    span = key_part.shape[1]
    key_heads = key_part.reshape(lat_n, span, H, head_dim)
    value_heads = value_part.reshape(lat_n, span, H, head_dim)
    scores = (
        jnp.einsum("aqhd,akhd->ahqk", query_heads, key_heads, preferred_element_type=jnp.float32)
        * score_scale
    )
    scores = scores + jnp.transpose(bias_part, (0, 2, 1)).astype(jnp.float32)[:, :, None, :]
    new_best = jnp.maximum(best, jnp.max(scores, axis=-1))
    weights = jnp.exp(scores - new_best[..., None])
    denom = jnp.sum(weights, axis=-1)
    accum = jnp.einsum(
        "ahqk,akhd->ahqd",
        weights.astype(jnp.bfloat16),
        value_heads,
        preferred_element_type=jnp.float32,
    )
    best, denom, accum = (new_best, denom, accum)
    attended = (
        jnp.transpose(accum / denom[..., None], (0, 2, 1, 3))
        .reshape(row_count, channels)
        .astype(jnp.bfloat16)
    )
    mixed = residual.astype(jnp.float32) + jnp.dot(
        attended, out_weight, preferred_element_type=jnp.float32
    )
    return mixed.astype(jnp.bfloat16).reshape(lat_n, lon_n, channels)


MESH = pl.DeviceIdType.MESH
EDGE = 16
PIECES = 2
OWN_SIB, EDGE_P, EDGE_Q, BIAS_SIB, BIAS_P, BIAS_Q = 0, 1, 2, 3, 4, 5
ATT_P, ATT_Q, ATT_SIB = 6, 7, 8
UNITS = ((0, 0), (0, 1), (1, 0), (1, 1))
CONV_P, CONV_SIB, CONV_FWD, UP, DOWN = 9, 13, 17, 21, 25
PIECE, PIECE_FWD = 29, 29 + PIECES
COPIES = 29 + 2 * PIECES


def block_kernel(
    lat_count,
    fields_ref,
    conv_ref,
    gain_ref,
    qkv_ref,
    outw_ref,
    bias_ref,
    out_ref,
    xbuf,
    conv_w,
    qkv_w,
    out_w,
    bias_all,
    bias_tile,
    part_send,
    part_recv,
    centre,
    cols,
    resid,
    normed,
    mixed,
    proj,
    att_send,
    att,
    send_sem,
    recv_sem,
    load_sem,
):
    n, channels = fields_ref.shape[1], fields_ref.shape[2]
    width = conv_ref.shape[1]
    half = 2 * n
    blocks = channels // width
    head_dim = channels // H
    me, row = lax.axis_index("lon"), lax.axis_index("lat")
    y, c = me // 2, me % 2
    sib, p, q = 2 * y + 1 - c, 2 * (1 - y) + c, 2 * (1 - y) + 1 - c
    above, below = row > 0, row < lat_count - 1

    def load(src, dst, idx):
        copy = pltpu.make_async_copy(src, dst, load_sem.at[idx])
        copy.start()
        return copy

    def remote(src, dst, idx, target):
        return pltpu.make_async_remote_copy(
            src_ref=src,
            dst_ref=dst,
            send_sem=send_sem.at[idx],
            recv_sem=recv_sem.at[idx],
            device_id=target,
            device_id_type=MESH,
        )

    def rows_at(offset, count):
        return pl.ds(pl.multiple_of(offset, EDGE), count)

    own = fields_ref.at[0]
    loads = [load(own, xbuf.at[0, rows_at(EDGE + c * n, n)], 0)]
    tap_rows = 3 * channels
    for idx, a in ((1, 2), (2, 0), (3, 1)):
        span = pl.ds(a * tap_rows, tap_rows)
        loads.append(load(conv_ref.at[span], conv_w.at[span], idx))
    for j in range(3):
        lanes = pl.ds(pl.multiple_of(j * channels + me * width, width), width)
        loads.append(load(qkv_ref.at[:, lanes], qkv_w.at[j], 4 + j))
    loads.append(load(outw_ref, out_w, 7))

    barrier = pltpu.get_barrier_semaphore()
    for other in (sib, p, q):
        pl.semaphore_signal(barrier, inc=1, device_id={"lon": other}, device_id_type=MESH)

    @pl.when(above)
    def _():
        pl.semaphore_signal(barrier, inc=1, device_id={"lat": row - 1}, device_id_type=MESH)

    @pl.when(below)
    def _():
        pl.semaphore_signal(barrier, inc=1, device_id={"lat": row + 1}, device_id_type=MESH)

    pl.semaphore_wait(barrier, 3 + above.astype(jnp.int32) + below.astype(jnp.int32))

    sends = []

    def begin(copy):
        copy.start()
        sends.append(copy)
        return copy

    edge_src = fields_ref.at[0, rows_at(c * (n - EDGE), EDGE)]
    edge_dst = xbuf.at[0, rows_at((1 - c) * (EDGE + half), EDGE)]
    edges = [
        begin(remote(edge_src, edge_dst, EDGE_P, {"lon": p})),
        begin(remote(edge_src, edge_dst, EDGE_Q, {"lon": q})),
    ]
    to_sib = begin(
        remote(own, xbuf.at[0, rows_at(EDGE + c * n, n)], OWN_SIB, {"lon": sib})
    )
    piece = n // PIECES
    pieces = [
        begin(
            remote(
                fields_ref.at[0, pl.ds(g * piece, piece)],
                xbuf.at[1, rows_at(EDGE + c * n + g * piece, piece)],
                PIECE + g,
                {"lon": p},
            )
        )
        for g in range(PIECES)
    ]
    biases = [
        begin(remote(bias_ref, bias_all.at[c], BIAS_SIB, {"lon": sib})),
        begin(remote(bias_ref, bias_all.at[2 + c], BIAS_P, {"lon": p})),
        begin(remote(bias_ref, bias_all.at[2 + c], BIAS_Q, {"lon": q})),
    ]
    bias_all[c] = bias_ref[...]

    def taps(k, a):
        full = EDGE + half + EDGE
        total = None
        for b in range(3):
            tap = 3 * a + b
            part = jnp.dot(
                xbuf[k],
                conv_w[tap * channels : (tap + 1) * channels],
                preferred_element_type=jnp.float32,
            )
            if b != 1:
                part = pltpu.roll(part, (1 - b) % full, 0)
            total = part if total is None else total + part
        return total[EDGE : EDGE + half]

    def unit_copies(first, make):
        return {u: make(first + i, *u) for i, u in enumerate(UNITS)}

    def part(k, side, h):
        span = pl.ds(h * n, n)
        return part_send.at[k, side, span], part_recv.at[k, side, span]

    def block(k, o, h):
        return cols.at[k, o, pl.ds(h * n, n)]

    up = unit_copies(UP, lambda idx, k, h: remote(*part(k, 0, h), idx, {"lat": row - 1}))
    down = unit_copies(DOWN, lambda idx, k, h: remote(*part(k, 1, h), idx, {"lat": row + 1}))
    conv_p = unit_copies(
        CONV_P, lambda idx, k, h: remote(block(k, me, h), block(1 - k, me, h), idx, {"lon": p})
    )
    conv_sib = unit_copies(
        CONV_SIB, lambda idx, k, h: remote(block(k, me, h), block(k, me, h), idx, {"lon": sib})
    )
    conv_fwd = unit_copies(
        CONV_FWD, lambda idx, k, h: remote(block(1 - k, p, h), block(1 - k, p, h), idx, {"lon": sib})
    )

    def send_part(k, side):
        part_send[k, side] = taps(k, 0 if side else 2).astype(jnp.bfloat16)

        @pl.when(below if side else above)
        def _():
            for h in range(2):
                (down if side else up)[k, h].start()

    def finish_conv(k, h):
        span = slice(h * n, (h + 1) * n)

        @pl.when(below)
        def _():
            up[k, h].wait_recv()
            centre[k, span] = centre[k, span] + part_recv[k, 0, span].astype(jnp.float32)

        @pl.when(above)
        def _():
            down[k, h].wait_recv()
            centre[k, span] = centre[k, span] + part_recv[k, 1, span].astype(jnp.float32)

        cols[k, me, span] = centre[k, span].astype(jnp.bfloat16)
        begin(conv_p[k, h])
        begin(conv_sib[k, h])

    loads[0].wait()
    to_sib.wait_recv()
    for copy in edges:
        copy.wait_recv()
    xbuf[1, 0:EDGE] = xbuf[0, half : half + EDGE]
    xbuf[1, EDGE + half : EDGE + half + EDGE] = xbuf[0, EDGE : EDGE + EDGE]
    loads[1].wait()
    send_part(0, 0)
    loads[2].wait()
    send_part(0, 1)
    loads[3].wait()
    centre[0] = taps(0, 1)

    forwards = []

    def pass_on(g):
        pieces[g].wait_recv()
        got = xbuf.at[1, rows_at(EDGE + c * n + g * piece, piece)]
        forwards.append(begin(remote(got, got, PIECE_FWD + g, {"lon": sib})))

    for g in range(PIECES - 1):
        pass_on(g)
    finish_conv(0, 0)
    finish_conv(0, 1)
    pass_on(PIECES - 1)
    for copy in forwards:
        copy.wait_recv()
    send_part(1, 0)
    send_part(1, 1)
    centre[1] = taps(1, 1)
    finish_conv(1, 0)
    finish_conv(1, 1)
    for h in range(2):
        conv_p[0, h].wait_recv()
        begin(conv_fwd[0, h])

    for j in range(3):
        loads[4 + j].wait()

    def project(k, h):
        span = slice(h * n, (h + 1) * n)
        squares = jnp.zeros((n, 1), jnp.float32)
        for o in range(blocks):
            lanes = slice(o * width, (o + 1) * width)
            summed = (
                xbuf[k, EDGE + h * n : EDGE + (h + 1) * n, lanes].astype(jnp.float32)
                + cols[k, o, span].astype(jnp.float32)
            ).astype(jnp.bfloat16)
            resid[k, span, lanes] = summed
            wide = summed.astype(jnp.float32)
            squares = squares + jnp.sum(wide * wide, axis=-1, keepdims=True)
        scale = lax.rsqrt(squares / channels + 1e-06)
        for o in range(blocks):
            lanes = slice(o * width, (o + 1) * width)
            normed[:, lanes] = (
                resid[k, span, lanes].astype(jnp.float32) * scale * gain_ref[:, lanes]
            ).astype(jnp.bfloat16)
        for j in range(3):
            proj[j, k * half + h * n : k * half + (h + 1) * n] = jnp.dot(
                normed[...], qkv_w[j], preferred_element_type=jnp.float32
            ).astype(jnp.bfloat16)

    for copy in biases:
        copy.wait_recv()
    lane = lax.broadcasted_iota(jnp.int32, (H, 2 * head_dim), 1)
    which = lax.broadcasted_iota(jnp.int32, (H, 2 * head_dim), 0)
    spread = jnp.where((lane == which) | (lane == which + head_dim), 1.0, 0.0).astype(jnp.bfloat16)
    for slot in range(4):
        bias_tile[slot * n : (slot + 1) * n] = lax.dot_general(
            bias_all[slot], spread, (((0,), (0,)), ((), ())), preferred_element_type=jnp.float32
        ).astype(jnp.bfloat16)

    for h in range(2):
        conv_sib[1, h].wait_recv()
        conv_fwd[0, h].wait_recv()
        project(1, h)
    for h in range(2):
        conv_p[1, h].wait_recv()
        begin(conv_fwd[1, h])
        conv_sib[0, h].wait_recv()
        conv_fwd[1, h].wait_recv()
        project(0, h)

    tile = 2 * head_dim
    score_scale = 1.0 / math.sqrt(head_dim)
    low_q = lax.broadcasted_iota(jnp.int32, (n, tile), 1)
    low_k = lax.broadcasted_iota(jnp.int32, (2 * half, tile), 1)

    def attend(offset, dst):
        for pair in range(width // tile):
            lanes = slice(pair * tile, (pair + 1) * tile)
            queries = proj[0, rows_at(offset, n), lanes].astype(jnp.float32) * score_scale
            keys, values = proj[1, :, lanes], proj[2, :, lanes]
            outs = []
            for odd in range(2):
                head = me * (width // head_dim) + 2 * pair + odd
                mine_q = (low_q >= head_dim) if odd else (low_q < head_dim)
                mine_k = (low_k >= head_dim) if odd else (low_k < head_dim)
                picked = jnp.where(low_q == head + (0 if odd else head_dim), 1.0, 0.0)
                q_ext = jnp.where(mine_q, queries, picked).astype(jnp.bfloat16)
                k_ext = jnp.where(mine_k, keys, bias_tile[...])
                scores = lax.dot_general(
                    q_ext, k_ext, (((1,), (1,)), ((), ())), preferred_element_type=jnp.float32
                )
                weights = jnp.exp(scores - jnp.max(scores, axis=-1, keepdims=True))
                total = jnp.sum(weights, axis=-1, keepdims=True)
                summed = jnp.dot(
                    weights.astype(jnp.bfloat16), values, preferred_element_type=jnp.float32
                )
                outs.append(summed / total)
            dst[:, lanes] = jnp.where(low_q < head_dim, outs[0], outs[1]).astype(jnp.bfloat16)

    attend(half + (1 - c) * n, att_send.at[0])
    att_q = begin(remote(att_send.at[0], att.at[me], ATT_Q, {"lon": q}))
    attend(half + c * n, att_send.at[1])
    att_p = begin(remote(att_send.at[1], att.at[me], ATT_P, {"lon": p}))
    attend((1 - c) * n, att_send.at[2])
    att_s = begin(remote(att_send.at[2], att.at[me], ATT_SIB, {"lon": sib}))
    attend(c * n, att.at[me])
    loads[7].wait()

    def mix(o):
        source = att[o]
        for j in range(blocks):
            lanes = slice(j * width, (j + 1) * width)
            mixed[:, lanes] = mixed[:, lanes] + jnp.dot(
                source,
                out_w[pl.ds(pl.multiple_of(o * width, width), width), lanes],
                preferred_element_type=jnp.float32,
            )

    mixed[...] = resid[0, rows_at(c * n, n)].astype(jnp.float32)
    mix(me)
    att_s.wait_recv()
    mix(sib)
    att_q.wait_recv()
    mix(q)
    att_p.wait_recv()
    mix(p)
    out_ref[0] = mixed[...].astype(jnp.bfloat16)

    for copy in sends:
        copy.wait_send()
    for u in UNITS:
        pl.when(above)(up[u].wait_send)
        pl.when(below)(down[u].wait_send)


def fused(fields, conv_weight, norm_gain, qkv_weight, out_weight, key_bias):
    _, n, channels = fields.shape
    width = conv_weight.shape[1]
    half = 2 * n
    lat_count = lax.axis_size("lat")
    lon_count = lax.axis_size("lon")
    head_dim = channels // H
    bf16, f32 = jnp.bfloat16, jnp.float32
    any_spec = pl.BlockSpec(memory_space=pl.ANY)
    vmem_spec = pl.BlockSpec(memory_space=pltpu.VMEM)
    return pl.pallas_call(
        functools.partial(block_kernel, lat_count),
        out_shape=jax.ShapeDtypeStruct(fields.shape, bf16),
        in_specs=[any_spec, any_spec, vmem_spec, any_spec, any_spec, vmem_spec],
        out_specs=vmem_spec,
        scratch_shapes=[
            pltpu.VMEM((2, half + 2 * EDGE, channels), bf16),
            pltpu.VMEM(conv_weight.shape, bf16),
            pltpu.VMEM((3, channels, width), bf16),
            pltpu.VMEM(out_weight.shape, bf16),
            pltpu.VMEM((4, H, n), bf16),
            pltpu.VMEM((2 * half, 2 * head_dim), bf16),
            pltpu.VMEM((2, 2, half, width), bf16),
            pltpu.VMEM((2, 2, half, width), bf16),
            pltpu.VMEM((2, half, width), f32),
            pltpu.VMEM((2, lon_count, half, width), bf16),
            pltpu.VMEM((2, half, channels), bf16),
            pltpu.VMEM((n, channels), bf16),
            pltpu.VMEM((n, channels), f32),
            pltpu.VMEM((3, 2 * half, width), bf16),
            pltpu.VMEM((3, n, width), bf16),
            pltpu.VMEM((lon_count, n, width), bf16),
            pltpu.SemaphoreType.DMA((COPIES,)),
            pltpu.SemaphoreType.DMA((COPIES,)),
            pltpu.SemaphoreType.DMA((8,)),
        ],
        compiler_params=pltpu.CompilerParams(
            collective_id=0, has_side_effects=True, vmem_limit_bytes=60 * 1024 * 1024
        ),
    )(fields, conv_weight, norm_gain.reshape(1, channels), qkv_weight, out_weight, key_bias[0].T)


def suits_kernel(fields, conv_weight):
    lat_n, n, channels = fields.shape
    width = conv_weight.shape[1]
    head_dim = channels // H
    return (
        lat_n == 1
        and lax.axis_size("lon") == 4
        and n % (EDGE * PIECES) == 0
        and width % 128 == 0
        and 2 * head_dim == 128
        and H <= head_dim
        and n * channels <= 2**18
    )


def per_device(fields, conv_weight, *others):
    if suits_kernel(fields, conv_weight):
        return fused(fields, conv_weight, *others)
    return on_device(fields, conv_weight, *others)


def solution(mesh):
    return jax.shard_map(
        per_device,
        mesh=mesh,
        in_specs=(
            P(("ens", "lat"), "lon", None),
            P(None, "lon"),
            P(),
            P(),
            P(),
            P("lat", "lon", None),
        ),
        out_specs=P(("ens", "lat"), "lon", None),
        check_vma=False,
    )
```
